32 devices in a mesh: groups: 2 (over y), rows: 16 (over z, x, core).
Axes of the slice: x: 2, y: 2, z: 4, core: 2. Of those that a mesh axis runs over, the one named last changes fastest.
Arguments:
- embeddings: float32 [16384, 4096], P(('groups', 'rows')), parts along dimension 0
- sketch: float32 [4096, 256], replicated, may hold values from -0.09375 to 0.09375
- pair_src: int32 [8192], P(('groups', 'rows')), parts along dimension 0, may hold values from 0 to 31, as said below
- pair_tgt: int32 [8192], P(('groups', 'rows')), parts along dimension 0, may hold values from 0 to 31, as said below
- pair_count: int32 [32], P(('groups', 'rows')), parts along dimension 0, may hold values from 64 to 256, as said below
Outputs:
- best_sim: float32 [16384], P(('groups', 'rows')), parts along dimension 0
The draws below stay inside these ranges and needn't reach their ends.
There are 2 independent parts, one for each index of `groups`. The reference program is written for one: setup_inputs(seed, part) draws one part's arguments, and reference() takes and returns one part's arrays. A program takes and returns all parts, laid end to end along the dimension named above; an argument that names none is the same for every part. Nothing has to cross between parts.
Inputs may be any that keep to these rules, and one draw needn't show every extreme that they name: `pair_src`: every slot of owner o names one of its own blocks, o * 2 to o * 2 + 1, and all slots of owner o whose target blocks lie on one index of rows name the same source block. `pair_tgt`: no slot of owner o names a block of o itself, and all slots of one owner that name blocks of one index of rows name the same block. `pair_count`: slots at or beyond an owner's count are not live.
All inputs are finite; a program needn't handle non-finite values.
Results may differ from the reference program's by a relative error of at most 0.00059.
Values may be sent and summed in bfloat16 or wider, within the bound.
A program may use at most 128 MiB of HBM per device.

```python
import math
import jax
import jax.numpy as jnp
from jax import lax

EMBED = 4096
SKETCH = 256
BLOCK = 256
BLK_DEV = 2
PAIRS_DEV = 256
BLOCKS = 32
ROWS = 8192
N_ROWS = 16


def pair_tables(key):
    subkeys = jax.random.split(key, 7)
    owner_ids = jnp.arange(N_ROWS, dtype=jnp.int32)
    spread = jax.random.randint(subkeys[0], (N_ROWS, PAIRS_DEV), 0, N_ROWS - 1)
    holder = (owner_ids[:, None] + 1 + spread) % N_ROWS
    block_table = jax.random.randint(subkeys[1], (N_ROWS, N_ROWS), 0, BLK_DEV)
    source_table = jax.random.randint(subkeys[2], (N_ROWS, N_ROWS), 0, BLK_DEV)
    within = jnp.take_along_axis(block_table, holder, axis=1)
    src_within = jnp.take_along_axis(source_table, holder, axis=1)
    src_block = owner_ids[:, None] * BLK_DEV + src_within
    tgt_block = holder * BLK_DEV + within
    crowded = jax.random.randint(subkeys[3], (N_ROWS,), 0, 8) == 0
    lighter = jax.random.randint(subkeys[4], (N_ROWS,), PAIRS_DEV // 4, PAIRS_DEV // 2 + 1)
    pair_total = jnp.where(crowded, PAIRS_DEV, lighter)
    fullest = jax.random.randint(subkeys[5], (), 0, N_ROWS)
    emptiest = (fullest + 1 + jax.random.randint(subkeys[6], (), 0, N_ROWS - 1)) % N_ROWS
    pair_total = jnp.where(owner_ids == fullest, PAIRS_DEV, pair_total)
    pair_total = jnp.where(owner_ids == emptiest, PAIRS_DEV // 4, pair_total)
    return (src_block.astype(jnp.int32), tgt_block.astype(jnp.int32), pair_total.astype(jnp.int32))


def draw_embeddings(key, part):
    src_block, tgt_block, pair_total = pair_tables(key)
    key = jax.random.fold_in(key, 11)
    subkeys = jax.random.split(key, 4)
    rows_dev = BLK_DEV * BLOCK
    base = jax.random.normal(subkeys[0], (ROWS, EMBED), jnp.float32)
    row_ids = jnp.arange(ROWS, dtype=jnp.int32)
    row_owner = row_ids // rows_dev
    row_block = row_ids // BLOCK
    slot_pick = jax.random.randint(subkeys[2], (ROWS,), 0, 1048576) % pair_total[row_owner]
    slot_src = src_block[row_owner, slot_pick]
    slot_tgt = tgt_block[row_owner, slot_pick]
    planted = slot_src == row_block
    partner = slot_tgt * BLOCK + jax.random.randint(subkeys[3], (ROWS,), 0, BLOCK)
    mixed = 0.6 * base + base[partner]
    return jnp.where(planted[:, None], mixed, base)


def draw_pair_src(key, part):
    return pair_tables(key)[0].reshape(-1)


def draw_pair_tgt(key, part):
    return pair_tables(key)[1].reshape(-1)


def draw_pair_count(key, part):
    return pair_tables(key)[2]


def normal_values(key, extent, scale, limit, held_as=jnp.bfloat16):
    array = jax.random.normal(key, extent, jnp.float32) * scale
    return jnp.minimum(jnp.maximum(array, -limit), limit).astype(held_as)


def setup_inputs(seed: int = 0, part: int = 0) -> dict:
    keys = jax.random.split(jax.random.key(seed), 6)
    part_splits = jax.random.split(jax.random.fold_in(keys[5], part), 6)
    embeddings = draw_embeddings(jax.random.fold_in(jax.random.fold_in(keys[5], part), 71), part)
    sketch = normal_values(keys[1], (EMBED, SKETCH), EMBED ** -0.5, 0.09375, jnp.float32)
    pair_src = draw_pair_src(jax.random.fold_in(jax.random.fold_in(keys[5], part), 71), part)
    pair_tgt = draw_pair_tgt(jax.random.fold_in(jax.random.fold_in(keys[5], part), 71), part)
    pair_count = draw_pair_count(jax.random.fold_in(jax.random.fold_in(keys[5], part), 71), part)
    return {"embeddings": embeddings, "sketch": sketch, "pair_src": pair_src, "pair_tgt": pair_tgt, "pair_count": pair_count}


def unit_rows(embeddings, sketch):
    sketched = jnp.dot(embeddings, sketch, precision=lax.Precision.HIGHEST, preferred_element_type=jnp.float32)
    width_total = sketched.shape[1]
    factor = lax.rsqrt(lax.optimization_barrier(jnp.mean(sketched * sketched, axis=1, keepdims=True)) + 1e-06) / math.sqrt(width_total)
    return (sketched * factor).astype(jnp.bfloat16)

def reference(embeddings, sketch, pair_src, pair_tgt, pair_count):
    normed = unit_rows(embeddings, sketch)
    blocks = normed.reshape(BLOCKS, BLOCK, SKETCH)
    src_all = pair_src.reshape(N_ROWS, PAIRS_DEV)
    tgt_all = pair_tgt.reshape(N_ROWS, PAIRS_DEV)
    owner_ids = jnp.arange(N_ROWS, dtype=jnp.int32)
    block_ids = jnp.arange(BLK_DEV, dtype=jnp.int32)

    def per_owner(col_state, owner_item):
        owner_index, sources, targets, pair_total = owner_item
        live_slots = jnp.arange(PAIRS_DEV, dtype=jnp.int32) < pair_total
        local_src = sources - owner_index * BLK_DEV
        holder = targets // BLK_DEV
        within = targets % BLK_DEV
        holder_hot = (holder[:, None] == owner_ids[None, :]) & live_slots[:, None]
        linked = jnp.any(holder_hot, axis=0)
        wanted = lax.optimization_barrier(jnp.max(jnp.where(holder_hot, within[:, None], -1), axis=0)).astype(jnp.int32)
        source_pick = lax.optimization_barrier(jnp.max(jnp.where(holder_hot, local_src[:, None], -1), axis=0)).astype(jnp.int32)
        chosen = (owner_ids * BLK_DEV + jnp.maximum(wanted, 0)).astype(jnp.int32)
        picked = (owner_index * BLK_DEV + jnp.maximum(source_pick, 0)).astype(jnp.int32)
        target_rows = blocks[chosen].astype(jnp.float32)
        source_rows = blocks[picked].astype(jnp.float32)
        scores = jnp.einsum('hrk,hck->hrc', source_rows, target_rows, precision=lax.Precision.HIGHEST)
        scores = jnp.where(linked[:, None, None], scores, -1.0)
        row_max = lax.optimization_barrier(jnp.max(scores, axis=2))
        col_max = lax.optimization_barrier(jnp.max(scores, axis=1))
        pick_hot = source_pick[:, None] == block_ids[None, :]
        row_best = lax.optimization_barrier(jnp.max(jnp.where(pick_hot[:, :, None], row_max[:, None, :], -1.0), axis=0))
        col_state = col_state.at[chosen].max(col_max)
        return (col_state, row_best)
    col_init = jnp.full((BLOCKS, BLOCK), -1.0, jnp.float32)
    col_state, row_best = lax.scan(per_owner, col_init, (owner_ids, src_all, tgt_all, pair_count))
    best_sim = jnp.maximum(row_best.reshape(BLOCKS, BLOCK), col_state)
    return jnp.maximum(best_sim, -1.0).reshape(ROWS)
```

```python
import functools
import math

import jax
import jax.numpy as jnp
from jax import lax
from jax.experimental import pallas as pl
from jax.experimental.pallas import tpu as pltpu
from jax.sharding import PartitionSpec as P

BLOCK = 256
K_TILE = 1024
NEG = -1.0


def chip_of(place, half):
    side = lax.div(place, half)
    return (place + side * (2 * half - 1 - 2 * place)) * 2 + side


def place_of(chip, half):
    side = lax.rem(chip, 2)
    level = lax.div(chip, 2)
    return level + side * (2 * half - 1 - 2 * level)


def kernel(
    device_count,
    chunk_rows,
    count_ref,
    src_ref,
    tgt_ref,
    emb_ref,
    sketch_ref,
    out_ref,
    emb,
    sketch,
    high,
    low,
    chain,
    mirror,
    best,
    emb_sem,
    sketch_sem,
    chain_send,
    chain_recv,
    mirror_send,
    mirror_recv,
):
    rows_dev, embed = emb.shape
    width = sketch.shape[1]
    chunk_count = rows_dev // chunk_rows
    chip_count = device_count // 2
    half = chip_count // 2
    blk_dev = rows_dev // BLOCK
    k_tile = min(K_TILE, embed)
    k_count = embed // k_tile

    emb_copies = [
        pltpu.make_async_copy(
            emb_ref.at[pl.ds(c * chunk_rows, chunk_rows)],
            emb.at[pl.ds(c * chunk_rows, chunk_rows)],
            emb_sem.at[c],
        )
        for c in range(chunk_count)
    ]
    sketch_copies = [
        pltpu.make_async_copy(
            sketch_ref.at[pl.ds(k * k_tile, k_tile)],
            sketch.at[pl.ds(k * k_tile, k_tile)],
            sketch_sem.at[k],
        )
        for k in range(k_count)
    ]
    emb_copies[0].start()
    for copy in sketch_copies:
        copy.start()
    for copy in emb_copies[1:]:
        copy.start()

    me = lax.axis_index("rows")
    core = lax.rem(me, 2)
    place = place_of(lax.div(me, 2), half)
    turn = 1 - 2 * core
    after = chip_of(lax.rem(place + turn + chip_count, chip_count), half) * 2 + core
    before = chip_of(lax.rem(place - turn + chip_count, chip_count), half) * 2 + core
    sibling = me + turn

    barrier = pltpu.get_barrier_semaphore()
    for other in (before, sibling):
        pl.semaphore_signal(
            barrier, inc=1, device_id={"rows": other}, device_id_type=pl.DeviceIdType.MESH
        )

    slots = src_ref.shape[1]
    live = lax.broadcasted_iota(jnp.int32, (1, slots), 1) < count_ref[0]
    local_src = src_ref[...] - me * blk_dev
    holder_first = lax.broadcasted_iota(jnp.int32, (device_count, slots), 0) * blk_dev
    codes = jnp.full((device_count, slots), -1, jnp.int32)
    for t in range(blk_dev):
        hit = (tgt_ref[...] == holder_first + t) & live
        codes = jnp.maximum(codes, jnp.where(hit, local_src * blk_dev + t, -1))
    codes = jnp.max(codes.astype(jnp.float32), axis=1, keepdims=True)
    chain[0, pl.ds(0, device_count), :] = jnp.broadcast_to(codes, (device_count, width)).astype(
        jnp.bfloat16
    )
    best[...] = jnp.full(best.shape, NEG, jnp.float32)

    def span(c):
        if c == 0:
            return pl.ds(0, device_count + chunk_rows)
        return pl.ds(device_count + c * chunk_rows, chunk_rows)

    def onward(hop, c):
        return pltpu.make_async_remote_copy(
            src_ref=chain.at[hop, span(c)],
            dst_ref=chain.at[hop + 1, span(c)],
            send_sem=chain_send.at[hop, c],
            recv_sem=chain_recv.at[hop, c],
            device_id={"rows": after},
            device_id_type=pl.DeviceIdType.MESH,
        )

    def across(hop, c):
        return pltpu.make_async_remote_copy(
            src_ref=chain.at[hop, span(c)],
            dst_ref=mirror.at[hop, span(c)],
            send_sem=mirror_send.at[hop, c],
            recv_sem=mirror_recv.at[hop, c],
            device_id={"rows": sibling},
            device_id_type=pl.DeviceIdType.MESH,
        )

    for c in range(chunk_count):
        emb_copies[c].wait()
        total = jnp.zeros((chunk_rows, width), jnp.float32)
        for k in range(k_count):
            depth = pl.ds(k * k_tile, k_tile)
            if c == 0:
                sketch_copies[k].wait()
                value = sketch[depth, :]
                top = value.astype(jnp.bfloat16)
                high[depth, :] = top
                low[depth, :] = (value - top.astype(jnp.float32)).astype(jnp.bfloat16)
            value = emb[pl.ds(c * chunk_rows, chunk_rows), depth]
            top = value.astype(jnp.bfloat16)
            rest = (value - top.astype(jnp.float32)).astype(jnp.bfloat16)
            total += jnp.dot(top, low[depth, :], preferred_element_type=jnp.float32)
            total += jnp.dot(rest, high[depth, :], preferred_element_type=jnp.float32)
            total += jnp.dot(top, high[depth, :], preferred_element_type=jnp.float32)
        mean = jnp.sum(total * total, axis=1, keepdims=True) * (1.0 / width)
        factor = lax.rsqrt(mean + 1e-06) * (1.0 / math.sqrt(width))
        chain[0, pl.ds(device_count + c * chunk_rows, chunk_rows), :] = (total * factor).astype(
            jnp.bfloat16
        )
        if c == 0:
            pl.semaphore_wait(barrier, 2)
        onward(0, c).start()
        across(0, c).start()

    def row_of(table, index):
        ids = lax.broadcasted_iota(jnp.int32, (device_count, width), 0)
        picked = jnp.where(ids == index, table.astype(jnp.float32), NEG)
        return jnp.max(picked, axis=0, keepdims=True)

    lane_block = lax.broadcasted_iota(jnp.int32, (1, rows_dev), 1)
    own_block = jnp.zeros((1, rows_dev), jnp.float32)
    for b in range(1, blk_dev):
        own_block += jnp.where(lane_block >= b * BLOCK, 1.0, 0.0)

    def score(held, hop, c, device):
        mine = row_of(chain[0, pl.ds(0, device_count), :], device)
        theirs = row_of(held[hop, pl.ds(0, device_count), :], me)
        repeat = rows_dev // width
        mine = jnp.concatenate([mine] * repeat, axis=1)
        theirs = jnp.concatenate([theirs] * repeat, axis=1)
        part = (c * chunk_rows) // BLOCK
        remote = held[hop, pl.ds(device_count + c * chunk_rows, chunk_rows), :]
        own = chain[0, pl.ds(device_count, rows_dev), :]
        tile = lax.dot_general(
            remote, own, (((1,), (1,)), ((), ())), preferred_element_type=jnp.float32
        )
        tile = jnp.max(tile.reshape(chunk_rows // 8, 8, rows_dev), axis=0)
        linked = (mine == own_block * blk_dev + part) | (theirs == own_block + part * blk_dev)
        best[...] = jnp.maximum(best[...], jnp.where(linked, tile, NEG))

    def chain_device(hop):
        return chip_of(lax.rem(place - turn * hop + chip_count, chip_count), half) * 2 + core

    def mirror_device(hop):
        return chip_of(lax.rem(place + turn * hop + chip_count, chip_count), half) * 2 + 1 - core

    def mirror_step(hop, c):
        across(hop, c).wait_recv()
        score(mirror, hop, c, mirror_device(hop))

    for c in range(chunk_count - 1):
        mirror_step(0, c)

    def hop_step(hop, last):
        for c in range(chunk_count):
            onward(hop - 1, c).wait_recv()
            if not last:
                onward(hop, c).start()
            across(hop, c).start()
            score(chain, hop, c, chain_device(hop))
            if c == 0:
                mirror_step(hop - 1, chunk_count - 1)
            else:
                mirror_step(hop, c - 1)

    def body(hop, carry):
        hop_step(hop, False)
        return carry

    lax.fori_loop(1, chip_count - 1, body, 0)
    hop_step(chip_count - 1, True)
    mirror_step(chip_count - 1, chunk_count - 1)
    out_ref[...] = jnp.max(best[...], axis=0, keepdims=True)

    def drain(hop, carry):
        for c in range(chunk_count):
            onward(hop, c).wait_send()
            across(hop, c).wait_send()
        return carry

    lax.fori_loop(0, chip_count - 1, drain, 0)
    for c in range(chunk_count):
        across(chip_count - 1, c).wait_send()


def per_device(embeddings, sketch, pair_src, pair_tgt, pair_count):
    device_count = lax.axis_size("rows")
    rows_dev, embed = embeddings.shape
    width = sketch.shape[1]
    chip_count = device_count // 2
    chunk_rows = 128 if chip_count <= 8 else 256
    chunks = rows_dev // chunk_rows
    item = (chip_count, device_count + rows_dev, width)
    slots = pair_src.shape[0]
    vmem = pl.BlockSpec(memory_space=pltpu.VMEM)
    best = pl.pallas_call(
        functools.partial(kernel, device_count, chunk_rows),
        out_shape=jax.ShapeDtypeStruct((1, rows_dev), jnp.float32),
        in_specs=[
            pl.BlockSpec(memory_space=pltpu.SMEM),
            vmem,
            vmem,
            pl.BlockSpec(memory_space=pl.ANY),
            pl.BlockSpec(memory_space=pl.ANY),
        ],
        out_specs=vmem,
        scratch_shapes=[
            pltpu.VMEM((rows_dev, embed), jnp.float32),
            pltpu.VMEM((embed, width), jnp.float32),
            pltpu.VMEM((embed, width), jnp.bfloat16),
            pltpu.VMEM((embed, width), jnp.bfloat16),
            pltpu.VMEM(item, jnp.bfloat16),
            pltpu.VMEM(item, jnp.bfloat16),
            pltpu.VMEM((8, rows_dev), jnp.float32),
            pltpu.SemaphoreType.DMA((chunks,)),
            pltpu.SemaphoreType.DMA((embed // min(K_TILE, embed),)),
            pltpu.SemaphoreType.DMA((chip_count, chunks)),
            pltpu.SemaphoreType.DMA((chip_count, chunks)),
            pltpu.SemaphoreType.DMA((chip_count, chunks)),
            pltpu.SemaphoreType.DMA((chip_count, chunks)),
        ],
        compiler_params=pltpu.CompilerParams(
            collective_id=0, has_side_effects=True, vmem_limit_bytes=60 * 1024 * 1024
        ),
    )(pair_count, pair_src.reshape(1, slots), pair_tgt.reshape(1, slots), embeddings, sketch)
    return best.reshape(rows_dev)


def solution(mesh):
    return jax.shard_map(
        per_device,
        mesh=mesh,
        in_specs=(
            P(("groups", "rows"), None),
            P(),
            P(("groups", "rows")),
            P(("groups", "rows")),
            P(("groups", "rows")),
        ),
        out_specs=P(("groups", "rows")),
        check_vma=False,
    )
```

```python
import functools
import math

import jax
import jax.numpy as jnp
from jax import lax
from jax.experimental import pallas as pl
from jax.experimental.pallas import tpu as pltpu
from jax.sharding import PartitionSpec as P

BLOCK = 256
K_TILE = 1024
NEG = -1.0


def chip_of(place, half):
    side = lax.div(place, half)
    return (place + side * (2 * half - 1 - 2 * place)) * 2 + side


def place_of(chip, half):
    side = lax.rem(chip, 2)
    level = lax.div(chip, 2)
    return level + side * (2 * half - 1 - 2 * level)


def kernel(
    device_count,
    chunk_rows,
    count_ref,
    src_ref,
    tgt_ref,
    emb_ref,
    sketch_ref,
    out_ref,
    emb,
    sketch,
    high,
    low,
    chain,
    mirror,
    best,
    emb_sem,
    sketch_sem,
    chain_send,
    chain_recv,
    mirror_send,
    mirror_recv,
):
    rows_dev, embed = emb.shape
    width = sketch.shape[1]
    chunk_count = rows_dev // chunk_rows
    chip_count = device_count // 2
    half = chip_count // 2
    blk_dev = rows_dev // BLOCK
    k_tile = min(K_TILE, embed)
    k_count = embed // k_tile

    emb_copies = [
        pltpu.make_async_copy(
            emb_ref.at[pl.ds(c * chunk_rows, chunk_rows)],
            emb.at[pl.ds(c * chunk_rows, chunk_rows)],
            emb_sem.at[c],
        )
        for c in range(chunk_count)
    ]
    sketch_copies = [
        pltpu.make_async_copy(
            sketch_ref.at[pl.ds(k * k_tile, k_tile)],
            sketch.at[pl.ds(k * k_tile, k_tile)],
            sketch_sem.at[k],
        )
        for k in range(k_count)
    ]
    for copy in sketch_copies:
        copy.start()
    for copy in emb_copies:
        copy.start()

    me = lax.axis_index("rows")
    core = lax.rem(me, 2)
    place = place_of(lax.div(me, 2), half)
    turn = 1 - 2 * core
    after = chip_of(lax.rem(place + turn + chip_count, chip_count), half) * 2 + core
    before = chip_of(lax.rem(place - turn + chip_count, chip_count), half) * 2 + core
    sibling = me + turn

    barrier = pltpu.get_barrier_semaphore()
    for other in (before, sibling):
        pl.semaphore_signal(
            barrier, inc=1, device_id={"rows": other}, device_id_type=pl.DeviceIdType.MESH
        )

    slots = src_ref.shape[1]
    live = lax.broadcasted_iota(jnp.int32, (1, slots), 1) < count_ref[0]
    local_src = src_ref[...] - me * blk_dev
    holder_first = lax.broadcasted_iota(jnp.int32, (device_count, slots), 0) * blk_dev
    codes = jnp.full((device_count, slots), -1, jnp.int32)
    for t in range(blk_dev):
        hit = (tgt_ref[...] == holder_first + t) & live
        codes = jnp.maximum(codes, jnp.where(hit, local_src * blk_dev + t, -1))
    codes = jnp.max(codes.astype(jnp.float32), axis=1, keepdims=True)
    chain[0, pl.ds(0, device_count), :] = jnp.broadcast_to(codes, (device_count, width)).astype(
        jnp.bfloat16
    )
    best[...] = jnp.full(best.shape, NEG, jnp.float32)

    def span(c):
        if c == 0:
            return pl.ds(0, device_count + chunk_rows)
        return pl.ds(device_count + c * chunk_rows, chunk_rows)

    def onward(hop, c):
        return pltpu.make_async_remote_copy(
            src_ref=chain.at[hop, span(c)],
            dst_ref=chain.at[hop + 1, span(c)],
            send_sem=chain_send.at[hop, c],
            recv_sem=chain_recv.at[hop, c],
            device_id={"rows": after},
            device_id_type=pl.DeviceIdType.MESH,
        )

    def across(hop, c):
        return pltpu.make_async_remote_copy(
            src_ref=chain.at[hop, span(c)],
            dst_ref=mirror.at[hop, span(c)],
            send_sem=mirror_send.at[hop, c],
            recv_sem=mirror_recv.at[hop, c],
            device_id={"rows": sibling},
            device_id_type=pl.DeviceIdType.MESH,
        )

    for c in range(chunk_count):
        emb_copies[c].wait()
        total = jnp.zeros((chunk_rows, width), jnp.float32)
        for k in range(k_count):
            depth = pl.ds(k * k_tile, k_tile)
            if c == 0:
                sketch_copies[k].wait()
                value = sketch[depth, :]
                top = value.astype(jnp.bfloat16)
                high[depth, :] = top
                low[depth, :] = (value - top.astype(jnp.float32)).astype(jnp.bfloat16)
            value = emb[pl.ds(c * chunk_rows, chunk_rows), depth]
            top = value.astype(jnp.bfloat16)
            rest = (value - top.astype(jnp.float32)).astype(jnp.bfloat16)
            total += jnp.dot(top, low[depth, :], preferred_element_type=jnp.float32)
            total += jnp.dot(rest, high[depth, :], preferred_element_type=jnp.float32)
            total += jnp.dot(top, high[depth, :], preferred_element_type=jnp.float32)
        mean = jnp.sum(total * total, axis=1, keepdims=True) * (1.0 / width)
        factor = lax.rsqrt(mean + 1e-06) * (1.0 / math.sqrt(width))
        chain[0, pl.ds(device_count + c * chunk_rows, chunk_rows), :] = (total * factor).astype(
            jnp.bfloat16
        )
        if c == 0:
            pl.semaphore_wait(barrier, 2)
        onward(0, c).start()
        across(0, c).start()

    def row_of(table, index):
        ids = lax.broadcasted_iota(jnp.int32, (device_count, width), 0)
        picked = jnp.where(ids == index, table.astype(jnp.float32), NEG)
        return jnp.max(picked, axis=0, keepdims=True)

    lane_block = lax.broadcasted_iota(jnp.int32, (1, rows_dev), 1)
    own_block = jnp.zeros((1, rows_dev), jnp.float32)
    for b in range(1, blk_dev):
        own_block += jnp.where(lane_block >= b * BLOCK, 1.0, 0.0)

    def score(held, hop, c, device):
        mine = row_of(chain[0, pl.ds(0, device_count), :], device)
        theirs = row_of(held[hop, pl.ds(0, device_count), :], me)
        repeat = rows_dev // width
        mine = jnp.concatenate([mine] * repeat, axis=1)
        theirs = jnp.concatenate([theirs] * repeat, axis=1)
        part = (c * chunk_rows) // BLOCK
        remote = held[hop, pl.ds(device_count + c * chunk_rows, chunk_rows), :]
        own = chain[0, pl.ds(device_count, rows_dev), :]
        tile = lax.dot_general(
            remote, own, (((1,), (1,)), ((), ())), preferred_element_type=jnp.float32
        )
        tile = jnp.max(tile.reshape(chunk_rows // 8, 8, rows_dev), axis=0)
        linked = (mine == own_block * blk_dev + part) | (theirs == own_block + part * blk_dev)
        best[...] = jnp.maximum(best[...], jnp.where(linked, tile, NEG))

    def chain_device(hop):
        return chip_of(lax.rem(place - turn * hop + chip_count, chip_count), half) * 2 + core

    def mirror_device(hop):
        return chip_of(lax.rem(place + turn * hop + chip_count, chip_count), half) * 2 + 1 - core

    def mirror_step(hop, c):
        across(hop, c).wait_recv()
        score(mirror, hop, c, mirror_device(hop))

    for c in range(chunk_count - 1):
        mirror_step(0, c)

    def hop_step(hop, last):
        for c in range(chunk_count):
            onward(hop - 1, c).wait_recv()
            if not last:
                onward(hop, c).start()
            across(hop, c).start()
            score(chain, hop, c, chain_device(hop))
            if c == 0:
                mirror_step(hop - 1, chunk_count - 1)
            else:
                mirror_step(hop, c - 1)

    def body(hop, carry):
        hop_step(hop, False)
        return carry

    lax.fori_loop(1, chip_count - 1, body, 0)
    hop_step(chip_count - 1, True)
    mirror_step(chip_count - 1, chunk_count - 1)
    out_ref[...] = best[...]

    def drain(hop, carry):
        for c in range(chunk_count):
            onward(hop, c).wait_send()
            across(hop, c).wait_send()
        return carry

    lax.fori_loop(0, chip_count - 1, drain, 0)
    for c in range(chunk_count):
        across(chip_count - 1, c).wait_send()


def per_device(embeddings, sketch, pair_src, pair_tgt, pair_count):
    device_count = lax.axis_size("rows")
    rows_dev, embed = embeddings.shape
    width = sketch.shape[1]
    chip_count = device_count // 2
    chunk_rows = 128 if chip_count <= 8 else 256
    chunks = rows_dev // chunk_rows
    item = (chip_count, device_count + rows_dev, width)
    slots = pair_src.shape[0]
    vmem = pl.BlockSpec(memory_space=pltpu.VMEM)
    best = pl.pallas_call(
        functools.partial(kernel, device_count, chunk_rows),
        out_shape=jax.ShapeDtypeStruct((8, rows_dev), jnp.float32),
        in_specs=[
            pl.BlockSpec(memory_space=pltpu.SMEM),
            vmem,
            vmem,
            pl.BlockSpec(memory_space=pl.ANY),
            pl.BlockSpec(memory_space=pl.ANY),
        ],
        out_specs=vmem,
        scratch_shapes=[
            pltpu.VMEM((rows_dev, embed), jnp.float32),
            pltpu.VMEM((embed, width), jnp.float32),
            pltpu.VMEM((embed, width), jnp.bfloat16),
            pltpu.VMEM((embed, width), jnp.bfloat16),
            pltpu.VMEM(item, jnp.bfloat16),
            pltpu.VMEM(item, jnp.bfloat16),
            pltpu.VMEM((8, rows_dev), jnp.float32),
            pltpu.SemaphoreType.DMA((chunks,)),
            pltpu.SemaphoreType.DMA((embed // min(K_TILE, embed),)),
            pltpu.SemaphoreType.DMA((chip_count, chunks)),
            pltpu.SemaphoreType.DMA((chip_count, chunks)),
            pltpu.SemaphoreType.DMA((chip_count, chunks)),
            pltpu.SemaphoreType.DMA((chip_count, chunks)),
        ],
        compiler_params=pltpu.CompilerParams(
            collective_id=0, has_side_effects=True, vmem_limit_bytes=60 * 1024 * 1024
        ),
    )(pair_count, pair_src.reshape(1, slots), pair_tgt.reshape(1, slots), embeddings, sketch)
    return jnp.max(best, axis=0)


def solution(mesh):
    return jax.shard_map(
        per_device,
        mesh=mesh,
        in_specs=(
            P(("groups", "rows"), None),
            P(),
            P(("groups", "rows")),
            P(("groups", "rows")),
            P(("groups", "rows")),
        ),
        out_specs=P(("groups", "rows")),
        check_vma=False,
    )
```
